32 devices in a mesh: groups: 2 (over x), loop: 16 (over z, y, core).
Axes of the slice: x: 2, y: 2, z: 4, core: 2. Of those that a mesh axis runs over, the one named last changes fastest.
Arguments:
- real: bfloat16 [32768, 256], P(('groups', 'loop')), parts along dimension 0, may hold values from -0.16 to 0.16
- generated: bfloat16 [32768, 256], P(('groups', 'loop')), parts along dimension 0, may hold values from -0.16 to 0.16
- real_potential: float32 [32768], P(('groups', 'loop')), parts along dimension 0, may hold values from 0.65 to 0.75
- generated_potential: float32 [32768], P(('groups', 'loop')), parts along dimension 0, may hold values from 0.65 to 0.75
Outputs:
- grad_real: bfloat16 [32768, 256], P(('groups', 'loop')), parts along dimension 0
- grad_generated: bfloat16 [32768, 256], P(('groups', 'loop')), parts along dimension 0
The draws below stay inside these ranges and needn't reach their ends.
There are 2 independent parts, one for each index of `groups`. The reference program is written for one: setup_inputs(seed, part) draws one part's arguments, and reference() takes and returns one part's arrays. A program takes and returns all parts, laid end to end along the dimension named above; each array names one. Nothing has to cross between parts.
All inputs are finite; a program needn't handle non-finite values.
Results may differ from the reference program's by a relative error of at most 0.0034.
Values may be sent and summed in bfloat16 or wider, within the bound.
A program may use at most 64 MiB of HBM per device.

```python
import jax
import jax.numpy as jnp
from jax import lax

D = 256
WINDOW = 4
ROWS_DEV = 1024
ROWS = 16384


def draw_real(key, part):
    key = jax.random.fold_in(key, 11)
    values = jnp.clip(0.04 * jax.random.normal(key, (ROWS, D), jnp.float32), -0.15625, 0.15625)
    return values.astype(jnp.bfloat16)


def draw_generated(key, part):
    key = jax.random.fold_in(key, 23)
    values = jnp.clip(0.04 * jax.random.normal(key, (ROWS, D), jnp.float32), -0.15625, 0.15625)
    return values.astype(jnp.bfloat16)


def shard_levels(rng, dims, pieces, least, high):
    gain = 1.0
    for axis_at, shards_of in pieces:
        draws = jax.random.uniform(jax.random.fold_in(jax.random.fold_in(rng, 6), axis_at), (shards_of,), jnp.float32, least / len(pieces), high / len(pieces))
        gain = gain * jnp.repeat(jnp.exp(draws), dims[axis_at] // shards_of).reshape((-1,) + (1,) * (len(dims) - 1 - axis_at))
    return gain


def setup_inputs(seed: int = 0, part: int = 0) -> dict:
    key_list = jax.random.split(jax.random.key(seed), 5)
    part_keys = jax.random.split(jax.random.fold_in(key_list[4], part), 5)
    real = draw_real(jax.random.fold_in(jax.random.fold_in(key_list[4], part), 71), part)
    generated = draw_generated(jax.random.fold_in(jax.random.fold_in(key_list[4], part), 71), part)
    real_potential = jnp.clip(0.65 + 0.100000024 * jax.random.uniform(part_keys[2], (ROWS,), jnp.float32) ** shard_levels(part_keys[2], (ROWS,), ((0, 16),), -0.2, 0.2), 0.65, 0.75)
    generated_potential = jnp.clip(0.65 + 0.100000024 * jax.random.uniform(part_keys[3], (ROWS,), jnp.float32) ** shard_levels(part_keys[3], (ROWS,), ((0, 16),), -0.2, 0.2), 0.65, 0.75)
    return {"real": real, "generated": generated, "real_potential": real_potential, "generated_potential": generated_potential}


epsilon = 0.05


def reference(real, generated, real_potential, generated_potential):
    blocks = ROWS // ROWS_DEV

    def step(gen_total, index):
        rstart = (index * ROWS_DEV).astype(jnp.int32)
        rows = lax.dynamic_slice_in_dim(real, rstart, ROWS_DEV, 0)
        rpot = lax.dynamic_slice_in_dim(real_potential, rstart, ROWS_DEV, 0)
        acc = jnp.zeros((ROWS_DEV, D), jnp.float32)
        for k in range(WINDOW):
            other = (index - k) % blocks
            start = (other * ROWS_DEV).astype(jnp.int32)
            points = lax.dynamic_slice_in_dim(generated, start, ROWS_DEV, 0)
            potential = lax.dynamic_slice_in_dim(generated_potential, start, ROWS_DEV, 0)
            inner = jnp.dot(rows, points.T, preferred_element_type=jnp.float32)
            kernel = jnp.exp((rpot[:, None] + potential[None, :] - 1.0 + inner) / epsilon).astype(jnp.bfloat16)
            acc = acc + jnp.dot(kernel, points, preferred_element_type=jnp.float32)
            column = jnp.dot(kernel.T, rows, preferred_element_type=jnp.float32)
            previous = lax.dynamic_slice_in_dim(gen_total, start, ROWS_DEV, 0)
            gen_total = lax.dynamic_update_slice_in_dim(gen_total, previous + column, start, 0)
        return gen_total, acc

    gen_total, totals = lax.scan(step, jnp.zeros((ROWS, D), jnp.float32), jnp.arange(blocks, dtype=jnp.int32))
    grad_real = (-totals.reshape(ROWS, D) / ROWS).astype(jnp.bfloat16)
    grad_generated = (-gen_total / ROWS).astype(jnp.bfloat16)
    return grad_real, grad_generated
```

```python
import functools

import jax
import jax.numpy as jnp
from jax import lax
from jax.experimental import pallas as pl
from jax.experimental.pallas import tpu as pltpu
from jax.sharding import PartitionSpec as P

WINDOW = 4
epsilon = 0.05
CHUNK = 256
TILE = 256


def kernel(
    n,
    real_ref, gen_ref, real_pot_ref, gen_pot_ref, out_real_ref, out_gen_ref,
    held, pots, columns, acc,
    load_sem, send_sem, recv_sem, pot_send_sem, pot_recv_sem,
):
    rows, width = real_ref.shape
    chunks = rows // CHUNK
    me = lax.axis_index("loop")
    odd = lax.rem(me, 2)
    mate = me + 1 - 2 * odd
    first, second = 1 - odd, odd

    loads = [
        pltpu.make_async_copy(gen_ref, held.at[0, 0], load_sem.at[0]),
        pltpu.make_async_copy(real_ref, held.at[1, 0], load_sem.at[1]),
    ]
    for load in loads:
        load.start()

    def other(distance):
        return lax.rem(me + distance + n, n)

    barrier = pltpu.get_barrier_semaphore()
    for distance in (1, 2, 3, -1, -2, -3):
        pl.semaphore_signal(
            barrier, inc=1, device_id={"loop": other(distance)},
            device_id_type=pl.DeviceIdType.MESH,
        )
    pots[0] = (gen_pot_ref[...] - 0.5) * (1.0 / epsilon)
    pots[4] = (real_pot_ref[...] - 0.5) * (1.0 / epsilon)
    for side in range(2):
        own = pots[4 * (1 - side)]
        columns[side] = jnp.transpose(jnp.broadcast_to(own, (128, rows)))
    acc[...] = jnp.zeros_like(acc)
    pl.semaphore_wait(barrier, 6)

    def block_copy(side, source, c, target, slot, kind):
        part = pl.ds(pl.multiple_of(c * CHUNK, CHUNK), CHUNK)
        return pltpu.make_async_remote_copy(
            src_ref=held.at[side, source, part],
            dst_ref=held.at[side, slot, part],
            send_sem=send_sem.at[side, kind, c],
            recv_sem=recv_sem.at[side, slot, c],
            device_id={"loop": target},
            device_id_type=pl.DeviceIdType.MESH,
        )

    def pot_copy(side, k):
        return pltpu.make_async_remote_copy(
            src_ref=pots.at[4 * side],
            dst_ref=pots.at[4 * side + k],
            send_sem=pot_send_sem.at[side, k - 1],
            recv_sem=pot_recv_sem.at[side, k - 1],
            device_id={"loop": other(k if side == 0 else -k)},
            device_id_type=pl.DeviceIdType.MESH,
        )

    def to_mate(c):
        return block_copy(second, 0, c, mate, 1, 1)

    def by_two(side, c):
        return block_copy(side, 0, c, other(2 - 4 * side), 2, 0)

    def by_three(c):
        return block_copy(first, 0, c, other(3 - 6 * first), 3, 1)

    def onward(which, c):
        if which == 0:
            return block_copy(first, 2, c, mate, 1, 2)
        return block_copy(second, 2, c, mate, 3, 2)

    for load in loads:
        load.wait()
    for side in range(2):
        for k in range(1, WINDOW):
            pot_copy(side, k).start()

    @pl.loop(0, chunks)
    def _(c):
        to_mate(c).start()
        by_two(0, c).start()
        by_two(1, c).start()
        by_three(c).start()

    def piece(side, slot, c):
        part = pl.ds(pl.multiple_of(c * CHUNK, CHUNK), CHUNK)
        points = held[side, slot, part]
        row = pots[4 * side + slot, :, part]
        for start in range(0, rows, TILE):
            tile = pl.ds(start, TILE)
            inner = lax.dot_general(
                held[1 - side, 0, tile], points, (((1,), (1,)), ((), ())),
                preferred_element_type=jnp.float32,
            )
            column = columns[side, tile]
            column = jnp.concatenate([column] * (CHUNK // 128), axis=1)
            weights = jnp.exp(inner * (1.0 / epsilon) + (column + row))
            acc[side, tile] += jnp.dot(
                weights.astype(jnp.bfloat16), points, preferred_element_type=jnp.float32
            )

    @pl.loop(0, chunks)
    def _(c):
        piece(0, 0, c)
        piece(1, 0, c)

    for side in range(2):
        for k in range(1, WINDOW):
            pot_copy(side, k).wait_recv()

    def arrived(side, slot, c):
        block_copy(side, 0, c, mate, slot, 0).wait_recv()

    @pl.loop(0, chunks)
    def _(c):
        arrived(first, 1, c)
        piece(first, 1, c)

    @pl.loop(0, chunks)
    def _(c):
        arrived(first, 2, c)
        onward(0, c).start()
        arrived(second, 2, c)
        onward(1, c).start()
        piece(first, 2, c)
        piece(second, 2, c)
        arrived(second, 3, c)
        piece(second, 3, c)
        arrived(second, 1, c)
        piece(second, 1, c)
        arrived(first, 3, c)
        piece(first, 3, c)

    scale = -1.0 / (rows * n)
    out_real_ref[...] = (acc[0] * scale).astype(out_real_ref.dtype)
    out_gen_ref[...] = (acc[1] * scale).astype(out_gen_ref.dtype)

    for side in range(2):
        for k in range(1, WINDOW):
            pot_copy(side, k).wait_send()

    @pl.loop(0, chunks)
    def _(c):
        to_mate(c).wait_send()
        by_two(0, c).wait_send()
        by_two(1, c).wait_send()
        by_three(c).wait_send()
        onward(0, c).wait_send()
        onward(1, c).wait_send()


def body(real, generated, real_potential, generated_potential):
    rows, width = real.shape
    n = lax.axis_size("loop")
    chunks = rows // CHUNK
    any_space = pl.BlockSpec(memory_space=pl.ANY)
    vmem = pl.BlockSpec(memory_space=pltpu.VMEM)
    out = jax.ShapeDtypeStruct((rows, width), jnp.bfloat16)
    pairs = 2 * WINDOW * rows * rows
    return pl.pallas_call(
        functools.partial(kernel, n),
        out_shape=(out, out),
        in_specs=[any_space, any_space, vmem, vmem],
        out_specs=(vmem, vmem),
        scratch_shapes=[
            pltpu.VMEM((2, WINDOW, rows, width), jnp.bfloat16),
            pltpu.VMEM((2 * WINDOW, 1, rows), jnp.float32),
            pltpu.VMEM((2, rows, 128), jnp.float32),
            pltpu.VMEM((2, rows, width), jnp.float32),
            pltpu.SemaphoreType.DMA((2,)),
            pltpu.SemaphoreType.DMA((2, 3, chunks)),
            pltpu.SemaphoreType.DMA((2, WINDOW, chunks)),
            pltpu.SemaphoreType.DMA((2, WINDOW - 1)),
            pltpu.SemaphoreType.DMA((2, WINDOW - 1)),
        ],
        compiler_params=pltpu.CompilerParams(
            collective_id=0, has_side_effects=True, vmem_limit_bytes=40 * 1024 * 1024
        ),
        cost_estimate=pl.CostEstimate(
            flops=4 * pairs * width, bytes_accessed=8 * rows * width, transcendentals=pairs
        ),
    )(real, generated, real_potential.reshape(1, rows), generated_potential.reshape(1, rows))


def solution(mesh):
    in_specs = (
        P(("groups", "loop"), None),
        P(("groups", "loop"), None),
        P(("groups", "loop")),
        P(("groups", "loop")),
    )
    out_specs = (P(("groups", "loop"), None), P(("groups", "loop"), None))
    return jax.shard_map(body, mesh=mesh, in_specs=in_specs, out_specs=out_specs, check_vma=False)
```

```python
import functools

import jax
import jax.numpy as jnp
from jax import lax
from jax.experimental import pallas as pl
from jax.experimental.pallas import tpu as pltpu
from jax.sharding import PartitionSpec as P

WINDOW = 4
epsilon = 0.05
CHUNK = 256
TILE = 256


def kernel(
    n,
    real_ref, gen_ref, real_pot_ref, gen_pot_ref, out_ref,
    held, raw, pots, columns, acc,
    load_sem, send_sem, recv_sem, pot_send_sem, pot_recv_sem,
):
    rows, width = real_ref.shape
    chunks = rows // CHUNK
    me = lax.axis_index("loop")
    odd = lax.rem(me, 2)
    mate = me + 1 - 2 * odd
    first, second = 1 - odd, odd

    loads = [
        pltpu.make_async_copy(gen_pot_ref, raw.at[0], load_sem.at[0]),
        pltpu.make_async_copy(real_pot_ref, raw.at[1], load_sem.at[1]),
        pltpu.make_async_copy(gen_ref, held.at[0, 0], load_sem.at[2]),
        pltpu.make_async_copy(real_ref, held.at[1, 0], load_sem.at[3]),
    ]
    for load in loads:
        load.start()

    def other(distance):
        return lax.rem(me + distance + n, n)

    barrier = pltpu.get_barrier_semaphore()
    for distance in (1, 2, 3, -1, -2, -3):
        pl.semaphore_signal(
            barrier, inc=1, device_id={"loop": other(distance)},
            device_id_type=pl.DeviceIdType.MESH,
        )
    loads[0].wait()
    loads[1].wait()
    pots[0] = (raw[0] - 0.5) * (1.0 / epsilon)
    pots[4] = (raw[1] - 0.5) * (1.0 / epsilon)
    pl.semaphore_wait(barrier, 6)

    def block_copy(side, c, target, slot, kind, source=None):
        part = pl.ds(pl.multiple_of(c * CHUNK, CHUNK), CHUNK)
        return pltpu.make_async_remote_copy(
            src_ref=held.at[side, 2, part] if source is None else source.at[part],
            dst_ref=held.at[side, slot, part],
            send_sem=send_sem.at[side, kind, c],
            recv_sem=recv_sem.at[side, slot, c],
            device_id={"loop": target},
            device_id_type=pl.DeviceIdType.MESH,
        )

    def pot_copy(side, k):
        return pltpu.make_async_remote_copy(
            src_ref=pots.at[4 * side],
            dst_ref=pots.at[4 * side + k],
            send_sem=pot_send_sem.at[side, k - 1],
            recv_sem=pot_recv_sem.at[side, k - 1],
            device_id={"loop": other(k if side == 0 else -k)},
            device_id_type=pl.DeviceIdType.MESH,
        )

    def by_two(side, c):
        return block_copy(side, c, other(2 - 4 * side), 2, 0, (gen_ref, real_ref)[side])

    def to_mate(side, c):
        return block_copy(side, c, mate, 1, 1, (gen_ref, real_ref)[side])

    def by_three(side, c):
        return block_copy(side, c, other(3 - 6 * side), 3, 1, (gen_ref, real_ref)[side])

    def onward(which, c):
        if which == 0:
            return block_copy(first, c, mate, 1, 2)
        return block_copy(second, c, mate, 3, 2)

    for side in range(2):
        for k in range(1, WINDOW):
            pot_copy(side, k).start()

    @pl.loop(0, chunks)
    def _(c):
        by_two(0, c).start()
        by_two(1, c).start()
        for side in range(2):

            @pl.when(second == side)
            def _():
                by_three(1 - side, c).start()
                to_mate(side, c).start()

    acc[...] = jnp.zeros_like(acc)
    for side in range(2):
        own = pots[4 * (1 - side)]
        columns[side] = jnp.transpose(jnp.broadcast_to(own, (128, rows)))
    loads[2].wait()
    loads[3].wait()

    scale = -1.0 / (rows * n)

    def piece(side, slot, c, last=False):
        part = pl.ds(pl.multiple_of(c * CHUNK, CHUNK), CHUNK)
        points = held[side, slot, part]
        row = pots[4 * side + slot, :, part]
        for start in range(0, rows, TILE):
            tile = pl.ds(start, TILE)
            inner = lax.dot_general(
                held[1 - side, 0, tile], points, (((1,), (1,)), ((), ())),
                preferred_element_type=jnp.float32,
            )
            column = columns[side, tile]
            column = jnp.concatenate([column] * (CHUNK // 128), axis=1)
            weights = jnp.exp(inner * (1.0 / epsilon) + (column + row))
            total = acc[side, tile] + jnp.dot(
                weights.astype(jnp.bfloat16), points, preferred_element_type=jnp.float32
            )
            if last:
                out_ref[side, tile] = (total * scale).astype(out_ref.dtype)
            else:
                acc[side, tile] = total

    @pl.loop(0, chunks)
    def _(c):
        piece(0, 0, c)
        piece(1, 0, c)

    for side in range(2):
        for k in range(1, WINDOW):
            pot_copy(side, k).wait_recv()

    def arrived(side, slot, c):
        block_copy(side, c, mate, slot, 0).wait_recv()

    @pl.loop(0, chunks)
    def _(c):
        arrived(first, 1, c)
        piece(first, 1, c)

    def round_of(c, last):
        arrived(first, 2, c)
        onward(0, c).start()
        arrived(second, 2, c)
        onward(1, c).start()
        arrived(second, 3, c)
        piece(second, 3, c)
        piece(first, 2, c)
        piece(second, 2, c)
        arrived(second, 1, c)
        piece(second, 1, c, last)
        arrived(first, 3, c)
        piece(first, 3, c, last)

    @pl.loop(0, chunks - 1)
    def _(c):
        round_of(c, False)

    round_of(chunks - 1, True)

    for side in range(2):
        for k in range(1, WINDOW):
            pot_copy(side, k).wait_send()

    @pl.loop(0, chunks)
    def _(c):
        by_two(0, c).wait_send()
        by_two(1, c).wait_send()
        for side in range(2):

            @pl.when(second == side)
            def _():
                by_three(1 - side, c).wait_send()
                to_mate(side, c).wait_send()

        onward(0, c).wait_send()
        onward(1, c).wait_send()


def hand_over(both_ref, real_ref, gen_ref, sem):
    copies = [
        pltpu.make_async_copy(both_ref.at[0], real_ref, sem.at[0]),
        pltpu.make_async_copy(both_ref.at[1], gen_ref, sem.at[1]),
    ]
    for copy in copies:
        copy.start()
    for copy in copies:
        copy.wait()


def body(real, generated, real_potential, generated_potential):
    rows, width = real.shape
    n = lax.axis_size("loop")
    chunks = rows // CHUNK
    operands = (
        real, generated, real_potential.reshape(1, rows), generated_potential.reshape(1, rows)
    )
    hbm = pl.BlockSpec(memory_space=pltpu.HBM)
    out = jax.ShapeDtypeStruct((rows, width), jnp.bfloat16)
    pairs = 2 * WINDOW * rows * rows
    both = pl.pallas_call(
        functools.partial(kernel, n),
        out_shape=pltpu.VMEM((2, rows, width), jnp.bfloat16),
        in_specs=[hbm] * 4,
        out_specs=pl.BlockSpec(memory_space=pltpu.VMEM),
        scratch_shapes=[
            pltpu.VMEM((2, WINDOW, rows, width), jnp.bfloat16),
            pltpu.VMEM((2, 1, rows), jnp.float32),
            pltpu.VMEM((2 * WINDOW, 1, rows), jnp.float32),
            pltpu.VMEM((2, rows, 128), jnp.float32),
            pltpu.VMEM((2, rows, width), jnp.float32),
            pltpu.SemaphoreType.DMA((4,)),
            pltpu.SemaphoreType.DMA((2, 3, chunks)),
            pltpu.SemaphoreType.DMA((2, WINDOW, chunks)),
            pltpu.SemaphoreType.DMA((2, WINDOW - 1)),
            pltpu.SemaphoreType.DMA((2, WINDOW - 1)),
        ],
        compiler_params=pltpu.CompilerParams(
            collective_id=0, has_side_effects=True, vmem_limit_bytes=24 * 1024 * 1024
        ),
        cost_estimate=pl.CostEstimate(
            flops=4 * pairs * width, bytes_accessed=8 * rows * width, transcendentals=pairs
        ),
    )(*(pltpu.with_memory_space_constraint(x, pltpu.HBM) for x in operands))
    return pl.pallas_call(
        hand_over,
        out_shape=(out, out),
        in_specs=[pl.BlockSpec(memory_space=pl.ANY)],
        out_specs=(hbm, hbm),
        scratch_shapes=[pltpu.SemaphoreType.DMA((2,))],
        compiler_params=pltpu.CompilerParams(vmem_limit_bytes=24 * 1024 * 1024),
    )(both)


def solution(mesh):
    in_specs = (
        P(("groups", "loop"), None),
        P(("groups", "loop"), None),
        P(("groups", "loop")),
        P(("groups", "loop")),
    )
    out_specs = (P(("groups", "loop"), None), P(("groups", "loop"), None))
    return jax.shard_map(body, mesh=mesh, in_specs=in_specs, out_specs=out_specs, check_vma=False)
```

```python
import functools

import jax
import jax.numpy as jnp
from jax import lax
from jax.experimental import pallas as pl
from jax.experimental.pallas import tpu as pltpu
from jax.sharding import PartitionSpec as P

WINDOW = 4
epsilon = 0.05
CHUNK = 256
TILE = 512


def kernel(
    n,
    real_ref, gen_ref, real_pot_ref, gen_pot_ref, out_ref,
    held, raw, pots, columns, acc,
    load_sem, send_sem, recv_sem, pot_send_sem, pot_recv_sem,
):
    rows, width = real_ref.shape
    chunks = rows // CHUNK
    me = lax.axis_index("loop")
    odd = lax.rem(me, 2)
    mate = me + 1 - 2 * odd
    first, second = 1 - odd, odd

    loads = [
        pltpu.make_async_copy(gen_pot_ref, raw.at[0], load_sem.at[0]),
        pltpu.make_async_copy(real_pot_ref, raw.at[1], load_sem.at[1]),
        pltpu.make_async_copy(gen_ref, held.at[0, 0], load_sem.at[2]),
        pltpu.make_async_copy(real_ref, held.at[1, 0], load_sem.at[3]),
    ]
    for load in loads:
        load.start()

    def other(distance):
        return lax.rem(me + distance + n, n)

    barrier = pltpu.get_barrier_semaphore()
    for distance in (1, 2, 3, -1, -2, -3):
        pl.semaphore_signal(
            barrier, inc=1, device_id={"loop": other(distance)},
            device_id_type=pl.DeviceIdType.MESH,
        )
    loads[0].wait()
    loads[1].wait()
    pots[0] = (raw[0] - 0.5) * (1.0 / epsilon)
    pots[4] = (raw[1] - 0.5) * (1.0 / epsilon)
    pl.semaphore_wait(barrier, 6)

    def block_copy(side, c, target, slot, kind, source=None):
        part = pl.ds(pl.multiple_of(c * CHUNK, CHUNK), CHUNK)
        return pltpu.make_async_remote_copy(
            src_ref=held.at[side, 2, part] if source is None else source.at[part],
            dst_ref=held.at[side, slot, part],
            send_sem=send_sem.at[side, kind, c],
            recv_sem=recv_sem.at[side, slot, c],
            device_id={"loop": target},
            device_id_type=pl.DeviceIdType.MESH,
        )

    def pot_copy(side, k):
        return pltpu.make_async_remote_copy(
            src_ref=pots.at[4 * side],
            dst_ref=pots.at[4 * side + k],
            send_sem=pot_send_sem.at[side, k - 1],
            recv_sem=pot_recv_sem.at[side, k - 1],
            device_id={"loop": other(k if side == 0 else -k)},
            device_id_type=pl.DeviceIdType.MESH,
        )

    def by_two(side, c):
        return block_copy(side, c, other(2 - 4 * side), 2, 0, (gen_ref, real_ref)[side])

    def to_mate(side, c):
        return block_copy(side, c, mate, 1, 1, (gen_ref, real_ref)[side])

    def by_three(side, c):
        return block_copy(side, c, other(3 - 6 * side), 3, 1, (gen_ref, real_ref)[side])

    def onward(which, c):
        if which == 0:
            return block_copy(first, c, mate, 1, 2)
        return block_copy(second, c, mate, 3, 2)

    for side in range(2):
        for k in range(1, WINDOW):
            pot_copy(side, k).start()

    @pl.loop(0, chunks)
    def _(c):
        for side in range(2):

            @pl.when(second == side)
            def _():
                by_three(1 - side, c).start()
                to_mate(side, c).start()

        by_two(0, c).start()
        by_two(1, c).start()

    acc[...] = jnp.zeros_like(acc)
    for side in range(2):
        own = pots[4 * (1 - side)]
        columns[side] = jnp.transpose(jnp.broadcast_to(own, (128, rows)))
    loads[2].wait()
    loads[3].wait()

    scale = -1.0 / (rows * n)

    def piece(side, slot, c, last=False):
        part = pl.ds(pl.multiple_of(c * CHUNK, CHUNK), CHUNK)
        points = held[side, slot, part]
        row = pots[4 * side + slot, :, part]

        def products(start):
            return lax.dot_general(
                held[1 - side, 0, pl.ds(start, TILE)], points, (((1,), (1,)), ((), ())),
                preferred_element_type=jnp.float32,
            )

        ahead = products(0)
        for start in range(0, rows, TILE):
            inner = ahead
            if start + TILE < rows:
                ahead = products(start + TILE)
            tile = pl.ds(start, TILE)
            column = columns[side, tile]
            column = jnp.concatenate([column] * (CHUNK // 128), axis=1)
            weights = jnp.exp(inner * (1.0 / epsilon) + (column + row))
            total = acc[side, tile] + jnp.dot(
                weights.astype(jnp.bfloat16), points, preferred_element_type=jnp.float32
            )
            if last:
                out_ref[side, tile] = (total * scale).astype(out_ref.dtype)
            else:
                acc[side, tile] = total

    @pl.loop(0, chunks)
    def _(c):
        piece(0, 0, c)
        piece(1, 0, c)

    for side in range(2):
        for k in range(1, WINDOW):
            pot_copy(side, k).wait_recv()

    def arrived(side, slot, c):
        block_copy(side, c, mate, slot, 0).wait_recv()

    @pl.loop(0, chunks)
    def _(c):
        arrived(first, 1, c)
        piece(first, 1, c)

    def round_of(c, last):
        arrived(first, 2, c)
        onward(0, c).start()
        arrived(second, 2, c)
        onward(1, c).start()
        if not last:
            arrived(second, 3, c)
            piece(second, 3, c)
        piece(first, 2, c)
        piece(second, 2, c)
        arrived(second, 1, c)
        piece(second, 1, c, last)
        arrived(first, 3, c)
        piece(first, 3, c, last)

    @pl.loop(0, chunks - 1)
    def _(c):
        round_of(c, False)

    arrived(second, 3, chunks - 1)
    piece(second, 3, chunks - 1)
    round_of(chunks - 1, True)

    for side in range(2):
        for k in range(1, WINDOW):
            pot_copy(side, k).wait_send()

    @pl.loop(0, chunks)
    def _(c):
        by_two(0, c).wait_send()
        by_two(1, c).wait_send()
        for side in range(2):

            @pl.when(second == side)
            def _():
                by_three(1 - side, c).wait_send()
                to_mate(side, c).wait_send()

        onward(0, c).wait_send()
        onward(1, c).wait_send()


def hand_over(both_ref, real_ref, gen_ref, sem):
    copies = [
        pltpu.make_async_copy(both_ref.at[0], real_ref, sem.at[0]),
        pltpu.make_async_copy(both_ref.at[1], gen_ref, sem.at[1]),
    ]
    for copy in copies:
        copy.start()
    for copy in copies:
        copy.wait()


def body(real, generated, real_potential, generated_potential):
    rows, width = real.shape
    n = lax.axis_size("loop")
    chunks = rows // CHUNK
    operands = (
        real, generated, real_potential.reshape(1, rows), generated_potential.reshape(1, rows)
    )
    hbm = pl.BlockSpec(memory_space=pltpu.HBM)
    out = jax.ShapeDtypeStruct((rows, width), jnp.bfloat16)
    pairs = 2 * WINDOW * rows * rows
    both = pl.pallas_call(
        functools.partial(kernel, n),
        out_shape=pltpu.VMEM((2, rows, width), jnp.bfloat16),
        in_specs=[hbm] * 4,
        out_specs=pl.BlockSpec(memory_space=pltpu.VMEM),
        scratch_shapes=[
            pltpu.VMEM((2, WINDOW, rows, width), jnp.bfloat16),
            pltpu.VMEM((2, 1, rows), jnp.float32),
            pltpu.VMEM((2 * WINDOW, 1, rows), jnp.float32),
            pltpu.VMEM((2, rows, 128), jnp.float32),
            pltpu.VMEM((2, rows, width), jnp.float32),
            pltpu.SemaphoreType.DMA((4,)),
            pltpu.SemaphoreType.DMA((2, 3, chunks)),
            pltpu.SemaphoreType.DMA((2, WINDOW, chunks)),
            pltpu.SemaphoreType.DMA((2, WINDOW - 1)),
            pltpu.SemaphoreType.DMA((2, WINDOW - 1)),
        ],
        compiler_params=pltpu.CompilerParams(
            collective_id=0, has_side_effects=True, vmem_limit_bytes=24 * 1024 * 1024
        ),
        cost_estimate=pl.CostEstimate(
            flops=4 * pairs * width, bytes_accessed=8 * rows * width, transcendentals=pairs
        ),
    )(*(pltpu.with_memory_space_constraint(x, pltpu.HBM) for x in operands))
    return pl.pallas_call(
        hand_over,
        out_shape=(out, out),
        in_specs=[pl.BlockSpec(memory_space=pl.ANY)],
        out_specs=(hbm, hbm),
        scratch_shapes=[pltpu.SemaphoreType.DMA((2,))],
        compiler_params=pltpu.CompilerParams(vmem_limit_bytes=24 * 1024 * 1024),
    )(both)


def solution(mesh):
    in_specs = (
        P(("groups", "loop"), None),
        P(("groups", "loop"), None),
        P(("groups", "loop")),
        P(("groups", "loop")),
    )
    out_specs = (P(("groups", "loop"), None), P(("groups", "loop"), None))
    return jax.shard_map(body, mesh=mesh, in_specs=in_specs, out_specs=out_specs, check_vma=False)
```
